512 devices in a mesh: feat: 8 (over z), vert: 64 (over y, x, core).
Axes of the slice: x: 4, y: 8, z: 8, core: 2. Of those that a mesh axis runs over, the one named last changes fastest.
Arguments:
- features: bfloat16 [49152, 1024], P('vert', 'feat'), may hold values from -6 to 6
- adjacency: bfloat16 [49152, 2304], P('vert'), may hold values from 0 to 2, as said below
- w_self: bfloat16 [1024, 256], P('feat'), may hold values from -0.1875 to 0.1875
- w_neigh: bfloat16 [1024, 256], P('feat'), may hold values from -0.375 to 0.375
- bias: float32 [256], replicated, may hold values from -3 to 3
- cotangent: bfloat16 [49152, 256], P('vert'), may hold values from -6 to 6
Outputs:
- hidden: bfloat16 [49152, 256], P('vert', 'feat')
- grad_features: bfloat16 [49152, 1024], P('vert', 'feat')
- grad_self: float32 [1024, 256], P('feat')
- grad_neigh: float32 [1024, 256], P('feat')
The draws below stay inside these ranges and needn't reach their ends.
Inputs may be any that keep to these rules, and one draw needn't show every extreme that they name: `adjacency`: entries are 0 or positive edge weights; a few per row are positive.
All inputs are finite; a program needn't handle non-finite values.
Results may differ from the reference program's by a relative error of at most 0.0053.
Values may be sent and summed in bfloat16 or wider, within the bound.
No kernel may reach another device: no remote copies, remote signals or barrier semaphores. Data moves between devices by JAX's collectives and lax.ppermute only.
A program may use at most 64 MiB of HBM per device.

```python
import math
import jax
import jax.numpy as jnp
from jax import lax

F = 1024
H = 256
VD = 768
VERTS = 49152
N_VERT = 64


def draw_adjacency(key, part):
    key = jax.random.fold_in(key, 7)
    first, second = jax.random.split(key)
    shape = (VERTS, 3 * VD)
    keep = jax.random.uniform(first, shape, jnp.float32) < 16.0 / (3 * VD)
    weight = jnp.exp(jax.random.uniform(second, shape, jnp.float32, math.log(0.25), math.log(2.0)))
    return jnp.where(keep, weight, 0.0).astype(jnp.bfloat16)


def levels(key, extent, cuts, least, largest):
    loudness, own = 1.0, jax.random.fold_in(key, 6)
    for dim, shards_of in cuts:
        draws = jnp.exp(jax.random.uniform(jax.random.fold_in(own, dim), (shards_of,), jnp.float32, least / len(cuts), largest / len(cuts)))
        loudness = loudness * jnp.repeat(draws, extent[dim] // shards_of).reshape([-1 if axis == dim else 1 for axis in range(len(extent))])
    return loudness


def bell_draw(key, extent, scale, limit, shards=(), kind=jnp.bfloat16):
    drawn = scale * jax.random.normal(key, extent, jnp.float32)
    if shards:
        drawn = drawn * levels(key, extent, shards, -0.22, 0.18)
    return jnp.clip(drawn, -limit, limit).astype(kind)


def setup_inputs(seed: int = 0) -> dict:
    arg_keys = jax.random.split(jax.random.key(seed), 7)
    features = bell_draw(arg_keys[0], (VERTS, F), 1.0, 6.0, ((0, 64), (1, 8)))
    adjacency = draw_adjacency(jax.random.fold_in(arg_keys[6], 71), 0)
    w_self = bell_draw(arg_keys[2], (F, H), F ** -0.5, 0.1875, ((0, 8),))
    w_neigh = bell_draw(arg_keys[3], (F, H), (F // 4) ** -0.5, 0.375, ((0, 8),))
    bias = bell_draw(arg_keys[4], (H,), 0.5, 3.0, (), jnp.float32)
    cotangent = bell_draw(arg_keys[5], (VERTS, H), 1.0, 6.0, ((0, 64),))
    return {"features": features, "adjacency": adjacency, "w_self": w_self, "w_neigh": w_neigh, "bias": bias, "cotangent": cotangent}


def reference(features, adjacency, w_self, w_neigh, bias, cotangent):
    slabs = adjacency.reshape(N_VERT, VD, 3 * VD)
    deg = 1.0 + jnp.sum(slabs.astype(jnp.float32), axis=2)
    padded = jnp.pad(features.reshape(N_VERT, VD, F), ((1, 1), (0, 0), (0, 0)))

    def forward(index):
        window = lax.dynamic_slice_in_dim(padded, index, 3, 0).reshape(3 * VD, F)
        tile = lax.dynamic_index_in_dim(slabs, index, 0, keepdims=False)
        weight = lax.dynamic_index_in_dim(deg, index, 0, keepdims=False)
        return (jnp.dot(tile, window, preferred_element_type=jnp.float32) / weight[:, None]).astype(jnp.bfloat16)

    order = jnp.arange(N_VERT, dtype=jnp.int32)
    agg = lax.map(forward, order).reshape(VERTS, F)
    pre = jnp.dot(features, w_self, preferred_element_type=jnp.float32) + jnp.dot(agg, w_neigh, preferred_element_type=jnp.float32) + bias.astype(jnp.float32)
    sig = jax.nn.sigmoid(pre)
    hidden = (pre * sig).astype(jnp.bfloat16)
    dpre = (cotangent.astype(jnp.float32) * sig * (1.0 + pre * (1.0 - sig))).astype(jnp.bfloat16)
    grad_self = jnp.dot(features.T, dpre, preferred_element_type=jnp.float32)
    grad_neigh = jnp.dot(agg.T, dpre, preferred_element_type=jnp.float32)
    scaled = (jnp.dot(dpre, w_neigh.T, preferred_element_type=jnp.float32) / deg.reshape(VERTS)[:, None]).astype(jnp.bfloat16)
    scaled_slabs = scaled.reshape(N_VERT, VD, F)

    def backward(index):
        tile = lax.dynamic_index_in_dim(slabs, index, 0, keepdims=False)
        part = lax.dynamic_index_in_dim(scaled_slabs, index, 0, keepdims=False)
        spread = lax.dot_general(tile, part, (((0,), (0,)), ((), ())), preferred_element_type=jnp.float32)
        return spread.reshape(3, VD, F)

    back = lax.map(backward, order)
    zero = jnp.zeros((1, VD, F), jnp.float32)
    from_next = jnp.concatenate([back[1:, 0], zero], axis=0)
    from_prev = jnp.concatenate([zero, back[:-1, 2]], axis=0)
    total = (back[:, 1] + from_next + from_prev).reshape(VERTS, F)
    grad_features = (jnp.dot(dpre, w_self.T, preferred_element_type=jnp.float32) + total).astype(jnp.bfloat16)
    return hidden, grad_features, grad_self, grad_neigh
```

```python
import jax
import jax.numpy as jnp
from jax import lax
from jax.sharding import Mesh, PartitionSpec as P

F32, BF16, F16 = jnp.float32, jnp.bfloat16, jnp.float16
Y, X, C = 8, 4, 2
VERT = ("y", "x", "c")


def contract(a, b, da, db):
    return lax.dot_general(a, b, (((da,), (db,)), ((), ())), preferred_element_type=F32)


def spread(block, axes, size):
    copies = jnp.broadcast_to(block[None], (size,) + block.shape)
    return lax.all_to_all(copies, axes, 0, 0, tiled=True)


def body(features, adjacency, w_self, w_neigh, bias, cotangent):
    rows, feats = features.shape
    hid = bias.shape[0]
    feat = lax.axis_size("z")
    width = hid // feat
    verts = Y * X * C
    up = [(i, i + 1) for i in range(verts - 1)]
    down = [(i + 1, i) for i in range(verts - 1)]

    before = lax.ppermute(features, VERT, up)
    after = lax.ppermute(features, VERT, down)
    deg = 1.0 + jnp.sum(adjacency.astype(F32), axis=1)
    window = jnp.concatenate([before, features, after], axis=0)
    agg = (contract(adjacency, window, 1, 0) / deg[:, None]).astype(BF16)
    partial = contract(w_self, features, 0, 1) + contract(w_neigh, agg, 0, 1)
    sent = (partial * 128.0).astype(F16).reshape(feat, width, rows)
    got = lax.all_to_all(sent, "z", 0, 0, tiled=True)
    offset = lax.axis_index("z") * width
    pre = jnp.sum(got.astype(F32), axis=0) * (1.0 / 128.0)
    pre = pre + lax.dynamic_slice_in_dim(bias, offset, width)[:, None]
    sig = jax.nn.sigmoid(pre)
    hidden = (pre * sig).astype(BF16).T

    upstream = lax.dynamic_slice_in_dim(cotangent, offset, width, 1).T.astype(F32)
    dpre_part = (upstream * sig * (1.0 + pre * (1.0 - sig))).astype(BF16)
    dpre = spread(dpre_part, "z", feat).reshape(hid, rows)

    grad = jnp.concatenate([contract(features, dpre, 0, 1), contract(agg, dpre, 0, 1)], axis=0)
    share = grad.shape[0] // (X * C)
    part = grad.astype(F16).reshape(X * C, share, hid)
    part = lax.all_to_all(part, ("x", "c"), 0, 0, tiled=True)
    part = jnp.sum(part.astype(F32), axis=0) * 0.25
    part = jnp.sum(spread(part.astype(F16), "y", Y).astype(F32), axis=0) * 0.125
    grad = spread(part.astype(F16), ("x", "c"), X * C).reshape(2 * feats, hid).astype(F32) * 32.0

    scaled = (contract(dpre, w_neigh, 0, 1) / deg[:, None]).astype(BF16)
    back = contract(adjacency, scaled, 0, 0)
    from_next = lax.ppermute((back[:rows] * 0.125).astype(F16), VERT, down)
    from_prev = lax.ppermute((back[2 * rows :] * 0.125).astype(F16), VERT, up)
    total = contract(dpre, w_self, 0, 1) + back[rows : 2 * rows]
    total = total + 8.0 * (from_next.astype(F32) + from_prev.astype(F32))
    return hidden, total.astype(BF16), grad[:feats], grad[feats:]


def solution(mesh):
    split = Mesh(mesh.devices.reshape(-1, Y, X, C), ("z",) + VERT)
    rows = P(VERT, None)
    return jax.shard_map(
        body,
        mesh=split,
        in_specs=(P(VERT, "z"), rows, P("z", None), P("z", None), P(), rows),
        out_specs=(P(VERT, "z"), P(VERT, "z"), P("z", None), P("z", None)),
        check_vma=False,
    )
```

```python
import jax
import jax.numpy as jnp
from jax import lax
from jax.experimental import pallas as pl
from jax.experimental.pallas import tpu as pltpu
from jax.sharding import Mesh, PartitionSpec as P

F32, BF16, F16 = jnp.float32, jnp.bfloat16, jnp.float16
Y, X, C = 8, 4, 2
VERT = ("y", "x", "c")
PARAMS = pltpu.CompilerParams(vmem_limit_bytes=16 * 1024 * 1024)
VMEM = pl.BlockSpec()
SMEM = pl.BlockSpec(memory_space=pltpu.SMEM)


def contract(a, b, da, db):
    return lax.dot_general(a, b, (((da,), (db,)), ((), ())), preferred_element_type=F32)


def mm(a, b):
    return jnp.dot(a, b, preferred_element_type=F32)


def exchange(blocks, axes):
    return lax.all_to_all(blocks, axes, 0, 0, tiled=True)


def exchange_down(blocks, axes):
    return lax.all_to_all(blocks, axes, 0, 0, tiled=True, axis_index_groups=[list(range(7, -1, -1))])


def swap_cores(block):
    return lax.ppermute(block, "c", [(0, 1), (1, 0)])


def swap_chips(block):
    pairs = [(i, i + 1) for i in range(1, Y * X * C - 1, 2)]
    return lax.ppermute(block, VERT, pairs + [(j, i) for i, j in pairs])


def side_kernel(even_ref, side_ref):
    side_ref[0] = even_ref[0]


def own_kernel(adj_ref, x_ref, ws_ref, wn_ref, own_ref, w_ref, wt_ref):
    rows = x_ref.shape[0]
    x = x_ref[...]
    wide = jnp.concatenate([x, jnp.ones_like(x)], axis=1)
    own_ref[...] = mm(adj_ref[:, rows : 2 * rows], wide)
    w = jnp.concatenate([ws_ref[...], wn_ref[...]], axis=0)
    w_ref[...] = w
    wt_ref[...] = w.T


def agg_kernel(even_ref, adj_ref, far_ref, near_ref, own_ref, x_ref, wt_ref, both_ref, deg_ref, part_ref):
    rows, feats = x_ref.shape
    even = even_ref[0] == 1
    far, near = far_ref[...], near_ref[...]
    ones = jnp.ones_like(far)
    before = jnp.concatenate([jnp.where(even, far, near), ones], axis=1)
    after = jnp.concatenate([jnp.where(even, near, far), ones], axis=1)
    total = own_ref[...] + mm(adj_ref[:, :rows], before) + mm(adj_ref[:, 2 * rows :], after)
    deg = 1.0 + total[:, feats:]
    deg_ref[...] = deg
    agg = (total[:, :feats] / deg).astype(BF16)
    both = jnp.concatenate([x_ref[...], agg], axis=1).T
    both_ref[...] = both
    part_ref[...] = mm(wt_ref[...], both) * 128.0


def act_kernel(pre_ref, bias_ref, up_ref, hidden_ref, dpre_ref):
    pre = pre_ref[...] * (1.0 / 128.0) + bias_ref[:, :1]
    sig = jax.nn.sigmoid(pre)
    hidden_ref[...] = pre * sig
    dpre = (up_ref[...].astype(F32) * sig * (1.0 + pre * (1.0 - sig))).astype(BF16)
    for i in range(dpre_ref.shape[0]):
        dpre_ref[i] = dpre


def gathered(ref):
    size = ref.shape[0] // 8
    return jnp.concatenate([ref[i * size : (i + 1) * size] for i in range(7, -1, -1)], axis=0)


def grad_kernel(both_ref, dpre_ref, grad_ref):
    grad_ref[...] = contract(both_ref[...], gathered(dpre_ref), 1, 1)


def back_kernel(adj_ref, deg_ref, w_ref, dpre_ref, first_ref, mid_ref, last_ref):
    rows, feats = mid_ref.shape
    dpre = gathered(dpre_ref)
    scaled = (mm(w_ref[feats:], dpre) / deg_ref[...]).astype(BF16)
    first_ref[...] = mm(scaled, adj_ref[:, :rows]).T
    last_ref[...] = mm(scaled, adj_ref[:, 2 * rows :]).T
    mid_ref[...] = (mm(scaled, adj_ref[:, rows : 2 * rows]) + mm(w_ref[:feats], dpre)).T


def cost(us):
    return pl.CostEstimate(flops=int(us * 1e9), bytes_accessed=0, transcendentals=0)


def body(features, adjacency, w_self, w_neigh, bias, cotangent):
    rows, feats = features.shape
    hid = bias.shape[0]
    feat = lax.axis_size("z")
    width = hid // feat
    even = lax.axis_index("c") == 0
    shape = jax.ShapeDtypeStruct

    far = swap_chips(features)
    near = swap_cores(features)
    side = pl.pallas_call(
        side_kernel,
        in_specs=[SMEM],
        out_specs=SMEM,
        out_shape=shape((1,), jnp.int32),
        cost_estimate=cost(5),
    )(even.astype(jnp.int32).reshape(1))
    own, w_both, w_flip = pl.pallas_call(
        own_kernel,
        in_specs=[VMEM] * 4,
        out_specs=[VMEM] * 3,
        out_shape=[shape((rows, 2 * feats), F32), shape((2 * feats, hid), BF16), shape((hid, 2 * feats), BF16)],
        compiler_params=PARAMS,
        cost_estimate=cost(3),
    )(adjacency, features, w_self, w_neigh)
    both, deg, part = pl.pallas_call(
        agg_kernel,
        in_specs=[SMEM] + [VMEM] * 6,
        out_specs=[VMEM] * 3,
        out_shape=[shape((2 * feats, rows), BF16), shape((rows, feats), F32), shape((hid, rows), F32)],
        compiler_params=PARAMS,
        cost_estimate=cost(3),
    )(side, adjacency, far, near, own, features, w_flip)
    offset = lax.axis_index("z") * width
    bias_part = jnp.broadcast_to(lax.dynamic_slice_in_dim(bias, offset, width)[:, None], (width, 128))
    upstream = lax.dynamic_slice_in_dim(cotangent, offset, width, 1).T
    deg = deg[:, 0][None]
    sent = part.astype(F16).reshape(feat, width, rows)
    sent, deg, upstream, bias_part = lax.optimization_barrier((sent, deg, upstream, bias_part))
    got = jnp.sum(exchange(sent, "z").astype(F32), axis=0)
    hidden, dpre = pl.pallas_call(
        act_kernel,
        in_specs=[VMEM] * 3,
        out_specs=[VMEM] * 2,
        out_shape=[shape((width, rows), F32), shape((feat, width, rows), BF16)],
        compiler_params=PARAMS,
        cost_estimate=cost(1),
    )(got, bias_part, upstream)
    dpre, hidden = lax.optimization_barrier((exchange_down(dpre, "z"), hidden))
    dpre = dpre.reshape(hid, rows)

    grad = pl.pallas_call(
        grad_kernel,
        in_specs=[VMEM] * 2,
        out_specs=VMEM,
        out_shape=shape((2 * feats, hid), F32),
        compiler_params=PARAMS,
        cost_estimate=cost(1),
    )(both, dpre)
    share = 2 * feats // (X * C)
    piece = grad.astype(F16).reshape(X * C, share, hid)
    piece = exchange_down(piece, ("x", "c"))
    piece = jnp.broadcast_to((jnp.sum(piece.astype(F32), axis=0) * 0.25).astype(F16), (Y, share, hid))
    piece = exchange_down(piece, "y")

    first, mid, last = pl.pallas_call(
        back_kernel,
        in_specs=[VMEM] * 4,
        out_specs=[VMEM] * 3,
        out_shape=[shape((rows, feats), F32)] * 3,
        compiler_params=PARAMS,
        cost_estimate=pl.CostEstimate(flops=6 * rows * rows * feats, bytes_accessed=6 * rows * rows, transcendentals=0),
    )(adjacency, deg, w_both, dpre)
    first = (first * 0.125).astype(F16)
    last = (last * 0.125).astype(F16)
    from_far = swap_chips(jnp.where(even, first, last))
    near = jnp.where(even, last, first)
    piece, near = lax.optimization_barrier((piece, near))
    piece = jnp.broadcast_to((jnp.sum(piece.astype(F32), axis=0) * 0.125).astype(F16), (X * C, share, hid))
    from_near = swap_cores(near)
    grad = exchange_down(piece, ("x", "c")).reshape(2 * feats, hid).astype(F32) * 32.0
    total = mid + 8.0 * (from_far.astype(F32) + from_near.astype(F32))
    return hidden.astype(BF16).T, total.astype(BF16), grad[:feats], grad[feats:]


def solution(mesh):
    split = Mesh(mesh.devices.reshape(-1, Y, X, C), ("z",) + VERT)
    rows = P(VERT, None)
    return jax.shard_map(
        body,
        mesh=split,
        in_specs=(P(VERT, "z"), rows, P("z", None), P("z", None), P(), rows),
        out_specs=(P(VERT, "z"), P(VERT, "z"), P("z", None), P("z", None)),
        check_vma=False,
    )
```

```python
import jax
import jax.numpy as jnp
from jax import lax
from jax.experimental import pallas as pl
from jax.experimental.pallas import tpu as pltpu
from jax.sharding import Mesh, PartitionSpec as P

F32, BF16, F16 = jnp.float32, jnp.bfloat16, jnp.float16
Y, X, C = 8, 4, 2
VERT = ("y", "x", "c")
PARAMS = pltpu.CompilerParams(vmem_limit_bytes=16 * 1024 * 1024)
VMEM = pl.BlockSpec()
SMEM = pl.BlockSpec(memory_space=pltpu.SMEM)


def contract(a, b, da, db):
    return lax.dot_general(a, b, (((da,), (db,)), ((), ())), preferred_element_type=F32)


def mm(a, b):
    return jnp.dot(a, b, preferred_element_type=F32)


def exchange(blocks, axes):
    return lax.all_to_all(blocks, axes, 0, 0, tiled=True)


def exchange_down(blocks, axes):
    return lax.all_to_all(blocks, axes, 0, 0, tiled=True, axis_index_groups=[list(range(7, -1, -1))])


def swap_cores(block):
    return lax.ppermute(block, "c", [(0, 1), (1, 0)])


def swap_chips(block):
    pairs = [(i, i + 1) for i in range(1, Y * X * C - 1, 2)]
    return lax.ppermute(block, VERT, pairs + [(j, i) for i, j in pairs])


def side_kernel(even_ref, side_ref):
    side_ref[0] = even_ref[0]


def wide(block):
    return jnp.concatenate([block, jnp.ones_like(block)], axis=1)


def near_kernel(even_ref, adj_ref, near_ref, x_ref, part_ref, far_ref, sem):
    rows = x_ref.shape[0]
    even = even_ref[0]
    at = pl.multiple_of((1 - even) * 2 * rows, rows)
    copy = pltpu.make_async_copy(adj_ref.at[:, pl.ds(at, rows)], far_ref, sem)
    copy.start()
    at = pl.multiple_of(even * rows, rows)
    near, x = near_ref[...], x_ref[...]
    pair = jnp.concatenate([jnp.where(even == 1, x, near), jnp.where(even == 1, near, x)], axis=0)
    part_ref[...] = mm(adj_ref[:, pl.ds(at, 2 * rows)], wide(pair))
    copy.wait()


def agg_kernel(adj_ref, far_ref, sum_ref, x_ref, ws_ref, wn_ref, both_ref, deg_ref, part_ref):
    feats = x_ref.shape[1]
    total = sum_ref[...] + mm(adj_ref[...], wide(far_ref[...]))
    deg = 1.0 + total[:, feats:]
    agg = (total[:, :feats] / deg).astype(BF16)
    both = jnp.concatenate([x_ref[...], agg], axis=1).T
    both_ref[...] = both
    weights = jnp.concatenate([ws_ref[...], wn_ref[...]], axis=0).T
    part_ref[...] = mm(weights, both) * 128.0
    deg_ref[...] = deg


def act_kernel(pre_ref, bias_ref, up_ref, hidden_ref, dpre_ref):
    pre = pre_ref[...] * (1.0 / 128.0) + bias_ref[:, :1]
    sig = jax.nn.sigmoid(pre)
    hidden_ref[...] = pre * sig
    dpre = (up_ref[...].astype(F32) * sig * (1.0 + pre * (1.0 - sig))).astype(BF16)
    for i in range(dpre_ref.shape[0]):
        dpre_ref[i] = dpre


def gathered(ref):
    size = ref.shape[0] // 8
    return jnp.concatenate([ref[i * size : (i + 1) * size] for i in range(7, -1, -1)], axis=0)


def grad_kernel(both_ref, dpre_ref, grad_ref):
    grad_ref[...] = contract(both_ref[...], gathered(dpre_ref), 1, 1)


def back_kernel(adj_ref, deg_ref, ws_ref, wn_ref, dpre_ref, first_ref, mid_ref, last_ref):
    rows, feats = mid_ref.shape
    dpre = gathered(dpre_ref)
    scaled = (mm(wn_ref[...], dpre) / deg_ref[...].T).astype(BF16)
    first_ref[...] = mm(scaled, adj_ref[:, :rows]).T
    last_ref[...] = mm(scaled, adj_ref[:, 2 * rows :]).T
    mid_ref[...] = (mm(scaled, adj_ref[:, rows : 2 * rows]) + mm(ws_ref[...], dpre)).T


def finish_kernel(grad_ref, mid_ref, halo_ref, total_ref, self_ref, neigh_ref):
    feats = self_ref.shape[0]
    total_ref[...] = (mid_ref[...] + halo_ref[...]).astype(BF16)
    self_ref[...] = grad_ref[:feats]
    neigh_ref[...] = grad_ref[feats:]


def cost(us):
    return pl.CostEstimate(flops=int(us * 1e9), bytes_accessed=0, transcendentals=0)


def body(features, adjacency, w_self, w_neigh, bias, cotangent):
    rows, feats = features.shape
    hid = bias.shape[0]
    feat = lax.axis_size("z")
    width = hid // feat
    even = lax.axis_index("c") == 0
    shape = jax.ShapeDtypeStruct

    far = swap_chips(features)
    near = swap_cores(features)
    side = pl.pallas_call(
        side_kernel,
        in_specs=[SMEM],
        out_specs=SMEM,
        out_shape=shape((1,), jnp.int32),
        cost_estimate=cost(5),
    )(even.astype(jnp.int32).reshape(1))
    summed, adj_far = pl.pallas_call(
        near_kernel,
        in_specs=[SMEM] + [VMEM] * 3,
        out_specs=[VMEM] * 2,
        out_shape=[shape((rows, 2 * feats), F32), shape((rows, rows), BF16)],
        scratch_shapes=[pltpu.SemaphoreType.DMA(())],
        compiler_params=PARAMS,
        cost_estimate=cost(2),
    )(side, adjacency, near, features)
    both, deg, part = pl.pallas_call(
        agg_kernel,
        in_specs=[VMEM] * 6,
        out_specs=[VMEM] * 3,
        out_shape=[shape((2 * feats, rows), BF16), shape((rows, feats), F32), shape((hid, rows), F32)],
        compiler_params=PARAMS,
        cost_estimate=cost(3),
    )(adj_far, far, summed, features, w_self, w_neigh)
    offset = lax.axis_index("z") * width
    bias_part = jnp.broadcast_to(lax.dynamic_slice_in_dim(bias, offset, width)[:, None], (width, 128))
    upstream = lax.dynamic_slice_in_dim(cotangent, offset, width, 1).T
    sent = part.astype(F16).reshape(feat, width, rows)
    sent, upstream, bias_part = lax.optimization_barrier((sent, upstream, bias_part))
    got = jnp.sum(exchange(sent, "z").astype(F32), axis=0)
    hidden, dpre = pl.pallas_call(
        act_kernel,
        in_specs=[VMEM] * 3,
        out_specs=[VMEM] * 2,
        out_shape=[shape((width, rows), F32), shape((feat, width, rows), BF16)],
        compiler_params=PARAMS,
        cost_estimate=cost(1),
    )(got, bias_part, upstream)
    dpre, hidden = lax.optimization_barrier((exchange_down(dpre, "z"), hidden))
    dpre = dpre.reshape(hid, rows)

    grad = pl.pallas_call(
        grad_kernel,
        in_specs=[VMEM] * 2,
        out_specs=VMEM,
        out_shape=shape((2 * feats, hid), F32),
        compiler_params=PARAMS,
        cost_estimate=cost(1),
    )(both, dpre)
    share = 2 * feats // (X * C)
    piece = grad.astype(F16).reshape(X * C, share, hid)
    piece = exchange_down(piece, ("x", "c"))
    piece = jnp.broadcast_to((jnp.sum(piece.astype(F32), axis=0) * 0.25).astype(F16), (Y, share, hid))
    piece = exchange_down(piece, "y")

    first, mid, last = pl.pallas_call(
        back_kernel,
        in_specs=[VMEM] * 5,
        out_specs=[VMEM] * 3,
        out_shape=[shape((rows, feats), F32)] * 3,
        compiler_params=PARAMS,
        cost_estimate=pl.CostEstimate(flops=6 * rows * rows * feats, bytes_accessed=6 * rows * rows, transcendentals=0),
    )(adjacency, deg, w_self, w_neigh, dpre)
    first = (first * 0.125).astype(F16)
    last = (last * 0.125).astype(F16)
    from_far = swap_chips(jnp.where(even, first, last))
    near = jnp.where(even, last, first)
    piece, near = lax.optimization_barrier((piece, near))
    piece = jnp.broadcast_to((jnp.sum(piece.astype(F32), axis=0) * 0.125).astype(F16), (X * C, share, hid))
    from_near = swap_cores(near)
    grad = exchange_down(piece, ("x", "c")).reshape(2 * feats, hid).astype(F32) * 32.0
    halo = 8.0 * (from_far.astype(F32) + from_near.astype(F32))
    total, grad_self, grad_neigh = pl.pallas_call(
        finish_kernel,
        out_shape=[shape((rows, feats), BF16), shape((feats, hid), F32), shape((feats, hid), F32)],
        compiler_params=PARAMS,
    )(grad, mid, halo)
    return hidden.astype(BF16).T, total, grad_self, grad_neigh


def solution(mesh):
    split = Mesh(mesh.devices.reshape(-1, Y, X, C), ("z",) + VERT)
    rows = P(VERT, None)
    return jax.shard_map(
        body,
        mesh=split,
        in_specs=(P(VERT, "z"), rows, P("z", None), P("z", None), P(), rows),
        out_specs=(P(VERT, "z"), P(VERT, "z"), P("z", None), P("z", None)),
        check_vma=False,
    )
```

```python
import jax
import jax.numpy as jnp
from jax import lax
from jax.experimental import pallas as pl
from jax.experimental.pallas import tpu as pltpu
from jax.sharding import Mesh, PartitionSpec as P

F32, BF16, F16 = jnp.float32, jnp.bfloat16, jnp.float16
Y, X, C = 8, 4, 2
VERT = ("y", "x", "c")
PARAMS = pltpu.CompilerParams(vmem_limit_bytes=16 * 1024 * 1024)
VMEM = pl.BlockSpec()


def contract(a, b, da, db):
    return lax.dot_general(a, b, (((da,), (db,)), ((), ())), preferred_element_type=F32)


def mm(a, b):
    return jnp.dot(a, b, preferred_element_type=F32)


def exchange(blocks, axes):
    return lax.all_to_all(blocks, axes, 0, 0, tiled=True)


def exchange_down(blocks, axes):
    return lax.all_to_all(blocks, axes, 0, 0, tiled=True, axis_index_groups=[list(range(7, -1, -1))])


def swap_cores(block):
    return lax.ppermute(block, "c", [(0, 1), (1, 0)])


def swap_chips(block):
    pairs = [(i, i + 1) for i in range(1, Y * X * C - 1, 2)]
    return lax.ppermute(block, VERT, pairs + [(j, i) for i, j in pairs])


def ones_kernel(ones_ref):
    ones_ref[...] = jnp.ones_like(ones_ref)


def slabs(adj_ref, first, count):
    rows = adj_ref.shape[0]
    return adj_ref[:, pl.ds(pl.multiple_of(first * rows, rows), count * rows)]


def far_kernel(adj_ref, far_ref, x_ref, ones_ref, cot_ref, sum_ref, up_ref, flipped):
    core, width = lax.axis_index("c"), up_ref.shape[0]
    far, x, ones = far_ref[...], x_ref[...], ones_ref[...]
    pair = jnp.concatenate([jnp.where(core == 0, far, x), jnp.where(core == 0, x, far)], axis=0)
    wide = jnp.concatenate([pair, jnp.concatenate([ones, ones], axis=0)], axis=1)
    sum_ref[...] = mm(slabs(adj_ref, core, 2), wide)
    flipped[...] = cot_ref[...].T
    up_ref[...] = flipped[pl.ds(pl.multiple_of(lax.axis_index("z") * width, width), width)]


def agg_kernel(adj_ref, near_ref, ones_ref, sum_ref, x_ref, ws_ref, wn_ref, bias_ref, both_ref, deg_ref, part_ref, column_ref, columns):
    feats = x_ref.shape[1]
    wide = jnp.concatenate([near_ref[...], ones_ref[...]], axis=1)
    total = sum_ref[...] + mm(slabs(adj_ref, 2 - 2 * lax.axis_index("c"), 1), wide)
    deg = 1.0 + total[:, feats:]
    agg = (total[:, :feats] / deg).astype(BF16)
    deg_ref[...] = deg.T[: deg_ref.shape[0]]
    both = jnp.concatenate([x_ref[...], agg], axis=1).T
    both_ref[...] = both
    weights = jnp.concatenate([ws_ref[...], wn_ref[...]], axis=0).T
    part_ref[...] = mm(weights, both) * 128.0
    width = column_ref.shape[0]
    columns[...] = jnp.broadcast_to(bias_ref[...], (columns.shape[1], columns.shape[0])).T
    column_ref[...] = columns[pl.ds(pl.multiple_of(lax.axis_index("z") * width, width), width)]


def act_kernel(pre_ref, bias_ref, up_ref, hidden_ref, dpre_ref):
    pre = pre_ref[...] * (1.0 / 128.0) + bias_ref[:, :1]
    sig = jax.nn.sigmoid(pre)
    hidden_ref[...] = pre * sig
    dpre = (up_ref[...].astype(F32) * sig * (1.0 + pre * (1.0 - sig))).astype(BF16)
    for i in range(dpre_ref.shape[0]):
        dpre_ref[i] = dpre


def gathered(ref):
    size = ref.shape[0] // 8
    return jnp.concatenate([ref[i * size : (i + 1) * size] for i in range(7, -1, -1)], axis=0)


def grad_kernel(both_ref, dpre_ref, grad_ref):
    grad_ref[...] = contract(both_ref[...], gathered(dpre_ref), 1, 1)


def back_kernel(adj_ref, deg_ref, ws_ref, wn_ref, dpre_ref, far_ref, near_ref, mid_ref):
    core = lax.axis_index("c")
    dpre = gathered(dpre_ref)
    scaled = (mm(wn_ref[...], dpre) / deg_ref[:1]).astype(BF16)

    def back(slab):
        return mm(scaled, slabs(adj_ref, slab, 1))

    far_ref[...] = back(2 * core).T
    near_ref[...] = back(2 - 2 * core).T
    mid_ref[...] = (back(1) + mm(ws_ref[...], dpre)).T


def finish_kernel(grad_ref, mid_ref, halo_ref, total_ref, self_ref, neigh_ref):
    feats = self_ref.shape[0]
    total_ref[...] = (mid_ref[...] + halo_ref[...]).astype(BF16)
    self_ref[...] = grad_ref[:feats]
    neigh_ref[...] = grad_ref[feats:]


def cost(us):
    return pl.CostEstimate(flops=int(us * 1e9), bytes_accessed=0, transcendentals=0)


def body(features, adjacency, w_self, w_neigh, bias, cotangent):
    rows, feats = features.shape
    hid = bias.shape[0]
    feat = lax.axis_size("z")
    width = hid // feat
    shape = jax.ShapeDtypeStruct

    far = swap_chips(features)
    near = swap_cores(features)
    ones = pl.pallas_call(
        ones_kernel, out_shape=shape((rows, feats), BF16), compiler_params=PARAMS, cost_estimate=cost(5)
    )()
    summed, upstream = pl.pallas_call(
        far_kernel,
        out_shape=[shape((rows, 2 * feats), F32), shape((width, rows), BF16)],
        scratch_shapes=[pltpu.VMEM((hid, rows), BF16)],
        compiler_params=PARAMS,
        cost_estimate=cost(2),
    )(adjacency, far, features, ones, cotangent)
    both, deg, part, bias_part = pl.pallas_call(
        agg_kernel,
        out_shape=[shape((2 * feats, rows), BF16), shape((8, rows), F32), shape((hid, rows), F32), shape((width, 128), F32)],
        scratch_shapes=[pltpu.VMEM((hid, 128), F32)],
        compiler_params=PARAMS,
        cost_estimate=cost(3),
    )(adjacency, near, ones, summed, features, w_self, w_neigh, bias[None])
    sent = part.astype(F16).reshape(feat, width, rows)
    sent, upstream, bias_part = lax.optimization_barrier((sent, upstream, bias_part))
    got = jnp.sum(exchange(sent, "z").astype(F32), axis=0)
    hidden, dpre = pl.pallas_call(
        act_kernel,
        in_specs=[VMEM] * 3,
        out_specs=[VMEM] * 2,
        out_shape=[shape((width, rows), F32), shape((feat, width, rows), BF16)],
        compiler_params=PARAMS,
        cost_estimate=cost(1),
    )(got, bias_part, upstream)
    dpre, hidden = lax.optimization_barrier((exchange_down(dpre, "z"), hidden))
    dpre = dpre.reshape(hid, rows)

    grad = pl.pallas_call(
        grad_kernel,
        in_specs=[VMEM] * 2,
        out_specs=VMEM,
        out_shape=shape((2 * feats, hid), F32),
        compiler_params=PARAMS,
        cost_estimate=cost(1),
    )(both, dpre)
    share = 2 * feats // (X * C)
    far, near, mid = pl.pallas_call(
        back_kernel,
        in_specs=[VMEM] * 5,
        out_specs=[VMEM] * 3,
        out_shape=[shape((rows, feats), F32)] * 3,
        compiler_params=PARAMS,
        cost_estimate=pl.CostEstimate(flops=6 * rows * rows * feats, bytes_accessed=6 * rows * rows, transcendentals=0),
    )(adjacency, deg, w_self, w_neigh, dpre)
    piece = grad.astype(F16).reshape(X * C, share, hid)
    piece, far, near, mid = lax.optimization_barrier((piece, far, near, mid))
    piece = exchange_down(piece, ("x", "c"))
    piece = jnp.broadcast_to((jnp.sum(piece.astype(F32), axis=0) * 0.25).astype(F16), (Y, share, hid))

    from_far = swap_chips((far * 0.125).astype(F16))
    piece, near, hidden = lax.optimization_barrier((exchange_down(piece, "y"), near, hidden))
    piece = jnp.broadcast_to((jnp.sum(piece.astype(F32), axis=0) * 0.125).astype(F16), (X * C, share, hid))
    from_near = swap_cores((near * 0.125).astype(F16))
    grad = exchange_down(piece, ("x", "c")).reshape(2 * feats, hid).astype(F32) * 32.0
    halo = 8.0 * (from_far.astype(F32) + from_near.astype(F32))
    total, grad_self, grad_neigh = pl.pallas_call(
        finish_kernel,
        out_shape=[shape((rows, feats), BF16), shape((feats, hid), F32), shape((feats, hid), F32)],
        compiler_params=PARAMS,
    )(grad, mid, halo)
    return hidden.astype(BF16).T, total, grad_self, grad_neigh


def solution(mesh):
    split = Mesh(mesh.devices.reshape(-1, Y, X, C), ("z",) + VERT)
    rows = P(VERT, None)
    return jax.shard_map(
        body,
        mesh=split,
        in_specs=(P(VERT, "z"), rows, P("z", None), P("z", None), P(), rows),
        out_specs=(P(VERT, "z"), P(VERT, "z"), P("z", None), P("z", None)),
        check_vma=False,
    )
```

```python
import jax
import jax.numpy as jnp
from jax import lax
from jax.experimental import pallas as pl
from jax.experimental.pallas import tpu as pltpu
from jax.sharding import Mesh, PartitionSpec as P

F32, BF16, F16 = jnp.float32, jnp.bfloat16, jnp.float16
Y, X, C = 8, 4, 2
VERT = ("y", "x", "c")
PARAMS = pltpu.CompilerParams(vmem_limit_bytes=16 * 1024 * 1024)
VMEM = pl.BlockSpec()


def contract(a, b, da, db):
    return lax.dot_general(a, b, (((da,), (db,)), ((), ())), preferred_element_type=F32)


def mm(a, b):
    return jnp.dot(a, b, preferred_element_type=F32)


def exchange(blocks, axes):
    return lax.all_to_all(blocks, axes, 0, 0, tiled=True)


def exchange_down(blocks, axes):
    return lax.all_to_all(blocks, axes, 0, 0, tiled=True, axis_index_groups=[list(range(7, -1, -1))])


def swap_cores(block):
    return lax.ppermute(block, "c", [(0, 1), (1, 0)])


def swap_chips(block):
    pairs = [(i, i + 1) for i in range(1, Y * X * C - 1, 2)]
    return lax.ppermute(block, VERT, pairs + [(j, i) for i, j in pairs])


def ones_kernel(ones_ref):
    ones_ref[...] = jnp.ones_like(ones_ref)


def slabs(adj_ref, first, count):
    rows = adj_ref.shape[0]
    return adj_ref[:, pl.ds(pl.multiple_of(first * rows, rows), count * rows)]


def own_kernel(adj_ref, x_ref, ones_ref, cot_ref, ws_ref, wn_ref, bias_ref, sum_ref, up_ref, w_ref, column_ref, turned, columns):
    width = up_ref.shape[0]
    here = pl.ds(pl.multiple_of(lax.axis_index("z") * width, width), width)
    sum_ref[...] = mm(slabs(adj_ref, 1, 1), jnp.concatenate([x_ref[...], ones_ref[...]], axis=1))
    turned[...] = cot_ref[...].T
    up_ref[...] = turned[here]
    w_ref[...] = jnp.concatenate([ws_ref[...], wn_ref[...]], axis=0).T
    columns[...] = jnp.broadcast_to(bias_ref[...], (columns.shape[1], columns.shape[0])).T
    column_ref[...] = columns[here]


def far_kernel(adj_ref, far_ref, ones_ref, own_ref, sum_ref):
    wide = jnp.concatenate([far_ref[...], ones_ref[...]], axis=1)
    sum_ref[...] = own_ref[...] + mm(slabs(adj_ref, 2 * lax.axis_index("c"), 1), wide)


def agg_kernel(adj_ref, near_ref, ones_ref, sum_ref, x_ref, w_ref, both_ref, deg_ref, part_ref):
    feats = x_ref.shape[1]
    wide = jnp.concatenate([near_ref[...], ones_ref[...]], axis=1)
    total = sum_ref[...] + mm(slabs(adj_ref, 2 - 2 * lax.axis_index("c"), 1), wide)
    deg = 1.0 + total[:, feats:]
    agg = (total[:, :feats] / deg).astype(BF16)
    deg_ref[...] = deg.T[: deg_ref.shape[0]]
    both = jnp.concatenate([x_ref[...], agg], axis=1).T
    both_ref[...] = both
    part_ref[...] = mm(w_ref[...], both) * 128.0


def act_kernel(pre_ref, bias_ref, up_ref, hidden_ref, dpre_ref):
    pre = pre_ref[...] * (1.0 / 128.0) + bias_ref[:, :1]
    sig = jax.nn.sigmoid(pre)
    hidden_ref[...] = pre * sig
    dpre = (up_ref[...].astype(F32) * sig * (1.0 + pre * (1.0 - sig))).astype(BF16)
    for i in range(dpre_ref.shape[0]):
        dpre_ref[i] = dpre


def gathered(ref):
    size = ref.shape[0] // 8
    return jnp.concatenate([ref[i * size : (i + 1) * size] for i in range(7, -1, -1)], axis=0)


def grad_kernel(both_ref, dpre_ref, grad_ref):
    grad_ref[...] = contract(both_ref[...], gathered(dpre_ref), 1, 1)


def back_kernel(adj_ref, deg_ref, ws_ref, wn_ref, dpre_ref, far_ref, near_ref, mid_ref):
    core = lax.axis_index("c")
    dpre = gathered(dpre_ref)
    scaled = (mm(wn_ref[...], dpre) / deg_ref[:1]).astype(BF16)

    def back(slab):
        return mm(scaled, slabs(adj_ref, slab, 1))

    far_ref[...] = back(2 * core).T
    near_ref[...] = back(2 - 2 * core).T
    mid_ref[...] = (back(1) + mm(ws_ref[...], dpre)).T


def finish_kernel(grad_ref, mid_ref, halo_ref, total_ref, self_ref, neigh_ref):
    feats = self_ref.shape[0]
    total_ref[...] = (mid_ref[...] + halo_ref[...]).astype(BF16)
    self_ref[...] = grad_ref[:feats]
    neigh_ref[...] = grad_ref[feats:]


def cost(us):
    return pl.CostEstimate(flops=int(us * 1e9), bytes_accessed=0, transcendentals=0)


def body(features, adjacency, w_self, w_neigh, bias, cotangent):
    rows, feats = features.shape
    hid = bias.shape[0]
    feat = lax.axis_size("z")
    width = hid // feat
    shape = jax.ShapeDtypeStruct

    far = swap_chips(features)
    near = swap_cores(features)
    ones = pl.pallas_call(
        ones_kernel, out_shape=shape((rows, feats), BF16), compiler_params=PARAMS, cost_estimate=cost(5)
    )()
    own, upstream, weights, bias_part = pl.pallas_call(
        own_kernel,
        out_shape=[
            shape((rows, 2 * feats), F32),
            shape((width, rows), BF16),
            shape((hid, 2 * feats), BF16),
            shape((width, 128), F32),
        ],
        scratch_shapes=[pltpu.VMEM((hid, rows), BF16), pltpu.VMEM((hid, 128), F32)],
        compiler_params=PARAMS,
        cost_estimate=cost(2),
    )(adjacency, features, ones, cotangent, w_self, w_neigh, bias[None])
    summed = pl.pallas_call(
        far_kernel, out_shape=shape((rows, 2 * feats), F32), compiler_params=PARAMS, cost_estimate=cost(2)
    )(adjacency, far, ones, own)
    both, deg, part = pl.pallas_call(
        agg_kernel,
        out_shape=[shape((2 * feats, rows), BF16), shape((8, rows), F32), shape((hid, rows), F32)],
        compiler_params=PARAMS,
        cost_estimate=cost(3),
    )(adjacency, near, ones, summed, features, weights)
    sent = part.astype(F16).reshape(feat, width, rows)
    sent, upstream, bias_part = lax.optimization_barrier((sent, upstream, bias_part))
    got = jnp.sum(exchange(sent, "z").astype(F32), axis=0)
    hidden, dpre = pl.pallas_call(
        act_kernel,
        in_specs=[VMEM] * 3,
        out_specs=[VMEM] * 2,
        out_shape=[shape((width, rows), F32), shape((feat, width, rows), BF16)],
        compiler_params=PARAMS,
        cost_estimate=cost(1),
    )(got, bias_part, upstream)
    dpre, hidden = lax.optimization_barrier((exchange_down(dpre, "z"), hidden))
    dpre = dpre.reshape(hid, rows)

    grad = pl.pallas_call(
        grad_kernel,
        in_specs=[VMEM] * 2,
        out_specs=VMEM,
        out_shape=shape((2 * feats, hid), F32),
        compiler_params=PARAMS,
        cost_estimate=cost(1),
    )(both, dpre)
    share = 2 * feats // (X * C)
    far, near, mid = pl.pallas_call(
        back_kernel,
        in_specs=[VMEM] * 5,
        out_specs=[VMEM] * 3,
        out_shape=[shape((rows, feats), F32)] * 3,
        compiler_params=PARAMS,
        cost_estimate=pl.CostEstimate(flops=6 * rows * rows * feats, bytes_accessed=6 * rows * rows, transcendentals=0),
    )(adjacency, deg, w_self, w_neigh, dpre)
    piece = grad.astype(F16).reshape(X * C, share, hid)
    piece, far, near, mid = lax.optimization_barrier((piece, far, near, mid))
    piece = exchange_down(piece, ("x", "c"))
    piece = jnp.broadcast_to((jnp.sum(piece.astype(F32), axis=0) * 0.25).astype(F16), (Y, share, hid))

    from_far = swap_chips((far * 0.125).astype(F16))
    piece, near, hidden = lax.optimization_barrier((exchange_down(piece, "y"), near, hidden))
    piece = jnp.broadcast_to((jnp.sum(piece.astype(F32), axis=0) * 0.125).astype(F16), (X * C, share, hid))
    from_near = swap_cores((near * 0.125).astype(F16))
    grad = exchange_down(piece, ("x", "c")).reshape(2 * feats, hid).astype(F32) * 32.0
    halo = 8.0 * (from_far.astype(F32) + from_near.astype(F32))
    total, grad_self, grad_neigh = pl.pallas_call(
        finish_kernel,
        out_shape=[shape((rows, feats), BF16), shape((feats, hid), F32), shape((feats, hid), F32)],
        compiler_params=PARAMS,
    )(grad, mid, halo)
    return hidden.astype(BF16).T, total, grad_self, grad_neigh


def solution(mesh):
    split = Mesh(mesh.devices.reshape(-1, Y, X, C), ("z",) + VERT)
    rows = P(VERT, None)
    return jax.shard_map(
        body,
        mesh=split,
        in_specs=(P(VERT, "z"), rows, P("z", None), P("z", None), P(), rows),
        out_specs=(P(VERT, "z"), P(VERT, "z"), P("z", None), P("z", None)),
        check_vma=False,
    )
```

```python
import jax
import jax.numpy as jnp
from jax import lax
from jax.experimental import pallas as pl
from jax.experimental.pallas import tpu as pltpu
from jax.sharding import Mesh, PartitionSpec as P

F32, BF16, F16 = jnp.float32, jnp.bfloat16, jnp.float16
Y, X, C = 8, 4, 2
VERT = ("y", "x", "c")
PARAMS = pltpu.CompilerParams(vmem_limit_bytes=16 * 1024 * 1024)
VMEM = pl.BlockSpec()


def contract(a, b, da, db):
    return lax.dot_general(a, b, (((da,), (db,)), ((), ())), preferred_element_type=F32)


def mm(a, b):
    return jnp.dot(a, b, preferred_element_type=F32)


def exchange(blocks, axes):
    return lax.all_to_all(blocks, axes, 0, 0, tiled=True)


def exchange_down(blocks, axes):
    return lax.all_to_all(blocks, axes, 0, 0, tiled=True, axis_index_groups=[list(range(7, -1, -1))])


def exchange_rows(blocks):
    return lax.all_to_all(blocks, "y", 0, 0, tiled=True, axis_index_groups=[[4, 5, 3, 6, 2, 7, 1, 0]])


def swap_cores(block):
    return lax.ppermute(block, "c", [(0, 1), (1, 0)])


def swap_chips(block):
    pairs = [(i, i + 1) for i in range(1, Y * X * C - 1, 2)]
    return lax.ppermute(block, VERT, pairs + [(j, i) for i, j in pairs])


def ones_kernel(ones_ref):
    ones_ref[...] = jnp.ones_like(ones_ref)


def slabs(adj_ref, first, count):
    rows = adj_ref.shape[0]
    return adj_ref[:, pl.ds(pl.multiple_of(first * rows, rows), count * rows)]


def own_kernel(adj_ref, x_ref, ones_ref, cot_ref, ws_ref, wn_ref, bias_ref, sum_ref, up_ref, w_ref, column_ref, turned, columns):
    width = up_ref.shape[0]
    here = pl.ds(pl.multiple_of(lax.axis_index("z") * width, width), width)
    sum_ref[...] = mm(slabs(adj_ref, 1, 1), jnp.concatenate([x_ref[...], ones_ref[...]], axis=1))
    turned[...] = cot_ref[...].T
    up_ref[...] = turned[here]
    w_ref[...] = jnp.concatenate([ws_ref[...], wn_ref[...]], axis=0).T
    columns[...] = jnp.broadcast_to(bias_ref[...], (columns.shape[1], columns.shape[0])).T
    column_ref[...] = columns[here]


def far_kernel(adj_ref, far_ref, ones_ref, own_ref, sum_ref):
    wide = jnp.concatenate([far_ref[...], ones_ref[...]], axis=1)
    sum_ref[...] = own_ref[...] + mm(slabs(adj_ref, 2 * lax.axis_index("c"), 1), wide)


def agg_kernel(adj_ref, near_ref, ones_ref, sum_ref, x_ref, w_ref, both_ref, deg_ref, part_ref):
    feats = x_ref.shape[1]
    wide = jnp.concatenate([near_ref[...], ones_ref[...]], axis=1)
    total = sum_ref[...] + mm(slabs(adj_ref, 2 - 2 * lax.axis_index("c"), 1), wide)
    deg = 1.0 + total[:, feats:]
    agg = (total[:, :feats] / deg).astype(BF16)
    deg_ref[...] = deg.T[: deg_ref.shape[0]]
    both = jnp.concatenate([x_ref[...], agg], axis=1).T
    both_ref[...] = both
    part_ref[...] = mm(w_ref[...], both) * 128.0


def act_kernel(pre_ref, bias_ref, up_ref, hidden_ref, dpre_ref):
    pre = pre_ref[...] * (1.0 / 128.0) + bias_ref[:, :1]
    sig = jax.nn.sigmoid(pre)
    hidden_ref[...] = pre * sig
    dpre = (up_ref[...].astype(F32) * sig * (1.0 + pre * (1.0 - sig))).astype(BF16)
    for i in range(dpre_ref.shape[0]):
        dpre_ref[i] = dpre


def gathered(ref):
    size = ref.shape[0] // 8
    return jnp.concatenate([ref[i * size : (i + 1) * size] for i in range(7, -1, -1)], axis=0)


def grad_kernel(both_ref, dpre_ref, grad_ref):
    grad_ref[...] = contract(both_ref[...], gathered(dpre_ref), 1, 1)


def back_kernel(adj_ref, deg_ref, ws_ref, wn_ref, dpre_ref, far_ref, near_ref, mid_ref):
    core = lax.axis_index("c")
    dpre = gathered(dpre_ref)
    scaled = (mm(wn_ref[...], dpre) / deg_ref[:1]).astype(BF16)

    def back(slab):
        return mm(scaled, slabs(adj_ref, slab, 1))

    far_ref[...] = back(2 * core).T
    near_ref[...] = back(2 - 2 * core).T
    mid_ref[...] = (back(1) + mm(ws_ref[...], dpre)).T


def finish_kernel(grad_ref, mid_ref, halo_ref, total_ref, self_ref, neigh_ref):
    feats = self_ref.shape[0]
    total_ref[...] = (mid_ref[...] + halo_ref[...]).astype(BF16)
    self_ref[...] = grad_ref[:feats]
    neigh_ref[...] = grad_ref[feats:]


def cost(us):
    return pl.CostEstimate(flops=int(us * 1e9), bytes_accessed=0, transcendentals=0)


def body(features, adjacency, w_self, w_neigh, bias, cotangent):
    rows, feats = features.shape
    hid = bias.shape[0]
    feat = lax.axis_size("z")
    width = hid // feat
    shape = jax.ShapeDtypeStruct

    far = swap_chips(features)
    near = swap_cores(features)
    ones = pl.pallas_call(
        ones_kernel, out_shape=shape((rows, feats), BF16), compiler_params=PARAMS, cost_estimate=cost(5)
    )()
    own, upstream, weights, bias_part = pl.pallas_call(
        own_kernel,
        out_shape=[
            shape((rows, 2 * feats), F32),
            shape((width, rows), BF16),
            shape((hid, 2 * feats), BF16),
            shape((width, 128), F32),
        ],
        scratch_shapes=[pltpu.VMEM((hid, rows), BF16), pltpu.VMEM((hid, 128), F32)],
        compiler_params=PARAMS,
        cost_estimate=cost(2),
    )(adjacency, features, ones, cotangent, w_self, w_neigh, bias[None])
    summed = pl.pallas_call(
        far_kernel, out_shape=shape((rows, 2 * feats), F32), compiler_params=PARAMS, cost_estimate=cost(2)
    )(adjacency, far, ones, own)
    both, deg, part = pl.pallas_call(
        agg_kernel,
        out_shape=[shape((2 * feats, rows), BF16), shape((8, rows), F32), shape((hid, rows), F32)],
        compiler_params=PARAMS,
        cost_estimate=cost(3),
    )(adjacency, near, ones, summed, features, weights)
    sent = part.astype(F16).reshape(feat, width, rows)
    sent, upstream, bias_part = lax.optimization_barrier((sent, upstream, bias_part))
    got = jnp.sum(exchange(sent, "z").astype(F32), axis=0)
    hidden, dpre = pl.pallas_call(
        act_kernel,
        in_specs=[VMEM] * 3,
        out_specs=[VMEM] * 2,
        out_shape=[shape((width, rows), F32), shape((feat, width, rows), BF16)],
        compiler_params=PARAMS,
        cost_estimate=cost(1),
    )(got, bias_part, upstream)
    dpre, hidden = lax.optimization_barrier((exchange_down(dpre, "z"), hidden))
    dpre = dpre.reshape(hid, rows)

    grad = pl.pallas_call(
        grad_kernel,
        in_specs=[VMEM] * 2,
        out_specs=VMEM,
        out_shape=shape((2 * feats, hid), F32),
        compiler_params=PARAMS,
        cost_estimate=cost(1),
    )(both, dpre)
    share = 2 * feats // (X * C)
    far, near, mid = pl.pallas_call(
        back_kernel,
        in_specs=[VMEM] * 5,
        out_specs=[VMEM] * 3,
        out_shape=[shape((rows, feats), F32)] * 3,
        compiler_params=PARAMS,
        cost_estimate=pl.CostEstimate(flops=6 * rows * rows * feats, bytes_accessed=6 * rows * rows, transcendentals=0),
    )(adjacency, deg, w_self, w_neigh, dpre)
    piece = grad.astype(F16).reshape(X * C, share, hid)
    piece, far, near, mid = lax.optimization_barrier((piece, far, near, mid))
    piece = exchange_down(piece, ("x", "c"))
    piece = jnp.broadcast_to((jnp.sum(piece.astype(F32), axis=0) * 0.25).astype(F16), (Y, share, hid))

    from_far = swap_chips((far * 0.125).astype(F16))
    piece, near, hidden = lax.optimization_barrier((exchange_rows(piece), near, hidden))
    piece = jnp.broadcast_to((jnp.sum(piece.astype(F32), axis=0) * 0.125).astype(F16), (X * C, share, hid))
    from_near = swap_cores((near * 0.125).astype(F16))
    grad = exchange_down(piece, ("x", "c")).reshape(2 * feats, hid).astype(F32) * 32.0
    halo = 8.0 * (from_far.astype(F32) + from_near.astype(F32))
    total, grad_self, grad_neigh = pl.pallas_call(
        finish_kernel,
        out_shape=[shape((rows, feats), BF16), shape((feats, hid), F32), shape((feats, hid), F32)],
        compiler_params=PARAMS,
    )(grad, mid, halo)
    return hidden.astype(BF16).T, total, grad_self, grad_neigh


def solution(mesh):
    split = Mesh(mesh.devices.reshape(-1, Y, X, C), ("z",) + VERT)
    rows = P(VERT, None)
    return jax.shard_map(
        body,
        mesh=split,
        in_specs=(P(VERT, "z"), rows, P("z", None), P("z", None), P(), rows),
        out_specs=(P(VERT, "z"), P(VERT, "z"), P("z", None), P("z", None)),
        check_vma=False,
    )
```

```python
import jax
import jax.numpy as jnp
from jax import lax
from jax.experimental import pallas as pl
from jax.experimental.pallas import tpu as pltpu
from jax.sharding import Mesh, PartitionSpec as P

F32, BF16, F16 = jnp.float32, jnp.bfloat16, jnp.float16
Y, X, C = 8, 4, 2
VERT = ("y", "x", "c")
PARAMS = pltpu.CompilerParams(vmem_limit_bytes=16 * 1024 * 1024)
VMEM = pl.BlockSpec()


def contract(a, b, da, db):
    return lax.dot_general(a, b, (((da,), (db,)), ((), ())), preferred_element_type=F32)


def mm(a, b):
    return jnp.dot(a, b, preferred_element_type=F32)


def exchange(blocks, axes):
    return lax.all_to_all(blocks, axes, 0, 0, tiled=True)


def exchange_down(blocks, axes):
    return lax.all_to_all(blocks, axes, 0, 0, tiled=True, axis_index_groups=[list(range(7, -1, -1))])


def exchange_rows(blocks):
    return lax.all_to_all(blocks, "y", 0, 0, tiled=True, axis_index_groups=[[4, 5, 3, 6, 2, 7, 1, 0]])


def swap_cores(block):
    return lax.ppermute(block, "c", [(0, 1), (1, 0)])


def swap_chips(block):
    pairs = [(i, i + 1) for i in range(1, Y * X * C - 1, 2)]
    return lax.ppermute(block, VERT, pairs + [(j, i) for i, j in pairs])


def ones_kernel(ones_ref):
    ones_ref[...] = jnp.ones_like(ones_ref)


def slabs(adj_ref, first, count):
    rows = adj_ref.shape[0]
    return adj_ref[:, pl.ds(pl.multiple_of(first * rows, rows), count * rows)]


def own_kernel(adj_ref, x_ref, ones_ref, cot_ref, ws_ref, wn_ref, bias_ref, sum_ref, up_ref, w_ref, column_ref, turned, columns):
    width = up_ref.shape[0]
    here = pl.ds(pl.multiple_of(lax.axis_index("z") * width, width), width)
    sum_ref[...] = mm(slabs(adj_ref, 1, 1), jnp.concatenate([x_ref[...], ones_ref[...]], axis=1))
    turned[...] = cot_ref[...].T
    up_ref[...] = turned[here]
    w_ref[...] = jnp.concatenate([ws_ref[...], wn_ref[...]], axis=0).T
    columns[...] = jnp.broadcast_to(bias_ref[...], (columns.shape[1], columns.shape[0])).T
    column_ref[...] = columns[here]


def far_kernel(adj_ref, far_ref, ones_ref, own_ref, sum_ref):
    wide = jnp.concatenate([far_ref[...], ones_ref[...]], axis=1)
    sum_ref[...] = own_ref[...] + mm(slabs(adj_ref, 2 * lax.axis_index("c"), 1), wide)


def agg_kernel(adj_ref, near_ref, ones_ref, sum_ref, x_ref, w_ref, both_ref, deg_ref, part_ref):
    feats = x_ref.shape[1]
    wide = jnp.concatenate([near_ref[...], ones_ref[...]], axis=1)
    total = sum_ref[...] + mm(slabs(adj_ref, 2 - 2 * lax.axis_index("c"), 1), wide)
    deg = 1.0 + total[:, feats:]
    agg = (total[:, :feats] / deg).astype(BF16)
    deg_ref[...] = deg.T[: deg_ref.shape[0]]
    both = jnp.concatenate([x_ref[...], agg], axis=1).T
    both_ref[...] = both
    part_ref[...] = mm(w_ref[...], both) * 128.0


def act_kernel(pre_ref, bias_ref, up_ref, hidden_ref, dpre_ref):
    pre = pre_ref[...] * (1.0 / 128.0) + bias_ref[:, :1]
    sig = jax.nn.sigmoid(pre)
    hidden_ref[...] = pre * sig
    dpre = (up_ref[...].astype(F32) * sig * (1.0 + pre * (1.0 - sig))).astype(BF16)
    for i in range(dpre_ref.shape[0]):
        dpre_ref[i] = dpre


def gathered(ref):
    size = ref.shape[0] // 8
    return jnp.concatenate([ref[i * size : (i + 1) * size] for i in range(7, -1, -1)], axis=0)


def grad_kernel(both_ref, dpre_ref, grad_ref):
    grad_ref[...] = contract(both_ref[...], gathered(dpre_ref), 1, 1)


def back_kernel(adj_ref, deg_ref, ws_ref, wn_ref, dpre_ref, far_ref, near_ref, mid_ref):
    core = lax.axis_index("c")
    dpre = gathered(dpre_ref)
    scaled = (mm(wn_ref[...], dpre) / deg_ref[:1]).astype(BF16)

    def back(slab):
        return mm(scaled, slabs(adj_ref, slab, 1))

    far_ref[...] = back(2 * core)
    near_ref[...] = back(2 - 2 * core)
    mid_ref[...] = back(1) + mm(ws_ref[...], dpre)


def finish_kernel(grad_ref, mid_ref, halo_ref, total_ref, self_ref, neigh_ref):
    feats = self_ref.shape[0]
    total_ref[...] = (mid_ref[...] + halo_ref[...]).T.astype(BF16)
    self_ref[...] = grad_ref[:feats]
    neigh_ref[...] = grad_ref[feats:]


def cost(us):
    return pl.CostEstimate(flops=int(us * 1e9), bytes_accessed=0, transcendentals=0)


def body(features, adjacency, w_self, w_neigh, bias, cotangent):
    rows, feats = features.shape
    hid = bias.shape[0]
    feat = lax.axis_size("z")
    width = hid // feat
    shape = jax.ShapeDtypeStruct

    far = swap_chips(features)
    near = swap_cores(features)
    ones = pl.pallas_call(
        ones_kernel, out_shape=shape((rows, feats), BF16), compiler_params=PARAMS, cost_estimate=cost(5)
    )()
    own, upstream, weights, bias_part = pl.pallas_call(
        own_kernel,
        out_shape=[
            shape((rows, 2 * feats), F32),
            shape((width, rows), BF16),
            shape((hid, 2 * feats), BF16),
            shape((width, 128), F32),
        ],
        scratch_shapes=[pltpu.VMEM((hid, rows), BF16), pltpu.VMEM((hid, 128), F32)],
        compiler_params=PARAMS,
        cost_estimate=cost(2),
    )(adjacency, features, ones, cotangent, w_self, w_neigh, bias[None])
    summed = pl.pallas_call(
        far_kernel, out_shape=shape((rows, 2 * feats), F32), compiler_params=PARAMS, cost_estimate=cost(2)
    )(adjacency, far, ones, own)
    both, deg, part = pl.pallas_call(
        agg_kernel,
        out_shape=[shape((2 * feats, rows), BF16), shape((8, rows), F32), shape((hid, rows), F32)],
        compiler_params=PARAMS,
        cost_estimate=cost(3),
    )(adjacency, near, ones, summed, features, weights)
    sent = part.astype(F16).reshape(feat, width, rows)
    sent, upstream, bias_part = lax.optimization_barrier((sent, upstream, bias_part))
    got = jnp.sum(exchange(sent, "z").astype(F32), axis=0)
    hidden, dpre = pl.pallas_call(
        act_kernel,
        in_specs=[VMEM] * 3,
        out_specs=[VMEM] * 2,
        out_shape=[shape((width, rows), F32), shape((feat, width, rows), BF16)],
        compiler_params=PARAMS,
        cost_estimate=cost(1),
    )(got, bias_part, upstream)
    dpre, hidden = lax.optimization_barrier((exchange_down(dpre, "z"), hidden))
    dpre = dpre.reshape(hid, rows)

    grad = pl.pallas_call(
        grad_kernel,
        in_specs=[VMEM] * 2,
        out_specs=VMEM,
        out_shape=shape((2 * feats, hid), F32),
        compiler_params=PARAMS,
        cost_estimate=cost(1),
    )(both, dpre)
    share = 2 * feats // (X * C)
    far, near, mid = pl.pallas_call(
        back_kernel,
        in_specs=[VMEM] * 5,
        out_specs=[VMEM] * 3,
        out_shape=[shape((feats, rows), F32)] * 3,
        compiler_params=PARAMS,
        cost_estimate=pl.CostEstimate(flops=6 * rows * rows * feats, bytes_accessed=6 * rows * rows, transcendentals=0),
    )(adjacency, deg, w_self, w_neigh, dpre)
    piece = grad.astype(F16).reshape(X * C, share, hid)
    piece, far, near, mid = lax.optimization_barrier((piece, far, near, mid))
    piece = exchange_down(piece, ("x", "c"))
    piece = jnp.broadcast_to((jnp.sum(piece.astype(F32), axis=0) * 0.25).astype(F16), (Y, share, hid))

    from_far = swap_chips((far * 0.125).astype(F16))
    piece, near, hidden = lax.optimization_barrier((exchange_rows(piece), near, hidden))
    piece = jnp.broadcast_to((jnp.sum(piece.astype(F32), axis=0) * 0.125).astype(F16), (X * C, share, hid))
    from_near = swap_cores((near * 0.125).astype(F16))
    grad = exchange_down(piece, ("x", "c")).reshape(2 * feats, hid).astype(F32) * 32.0
    halo = 8.0 * (from_far.astype(F32) + from_near.astype(F32))
    total, grad_self, grad_neigh = pl.pallas_call(
        finish_kernel,
        out_shape=[shape((rows, feats), BF16), shape((feats, hid), F32), shape((feats, hid), F32)],
        compiler_params=PARAMS,
    )(grad, mid, halo)
    return hidden.astype(BF16).T, total, grad_self, grad_neigh


def solution(mesh):
    split = Mesh(mesh.devices.reshape(-1, Y, X, C), ("z",) + VERT)
    rows = P(VERT, None)
    return jax.shard_map(
        body,
        mesh=split,
        in_specs=(P(VERT, "z"), rows, P("z", None), P("z", None), P(), rows),
        out_specs=(P(VERT, "z"), P(VERT, "z"), P("z", None), P("z", None)),
        check_vma=False,
    )
```
